32 devices in a mesh: frame: 8 (over y, x, core), head: 4 (over z).
Axes of the slice: x: 2, y: 2, z: 4, core: 2. Of those that a mesh axis runs over, the one named last changes fastest.
Arguments:
- query_states: bfloat16 [4096, 1024], P('frame', 'head'), may hold values from -4.6 to 4.6
- key_states: bfloat16 [4096, 1024], P('frame', 'head'), may hold values from -4.6 to 4.6
- value_states: bfloat16 [4096, 1024], P('frame', 'head'), may hold values from -24 to 24
- out_weight: bfloat16 [1024, 5120], P('head'), may hold values from -0.1875 to 0.1875
- upstream: bfloat16 [4096, 5120], P('frame'), may hold values from -72 to 72
- tile_mask: int32 [16, 5], replicated, may hold values from 0 to 1, as said below
Outputs:
- attended: bfloat16 [4096, 1024], P('frame', 'head')
- projected: bfloat16 [4096, 5120], P('frame', 'head')
- grad_query: bfloat16 [4096, 1024], P('frame', 'head')
- grad_key: bfloat16 [4096, 1024], P('frame', 'head')
- grad_value: bfloat16 [4096, 1024], P('frame', 'head')
- gram_left: float32 [8, 16, 128, 128], P('head', 'frame')
- gram_right: float32 [8, 16, 320, 320], P('head', 'frame')
The draws below stay inside these ranges and needn't reach their ends.
Inputs may be any that keep to these rules, and one draw needn't show every extreme that they name: `tile_mask`: in every row, column 2 (the query tile's own tile) is 1.
All inputs are finite; a program needn't handle non-finite values.
Results may differ from the reference program's by a relative error of at most 0.019.
Values may be sent and summed in bfloat16 or wider, within the bound.
A program may use at most 128 MiB of HBM per device.

```python
import math
import jax
import jax.numpy as jnp
from jax import lax

D = 5120
HD = 128
HEAD_DEV = 2
TILE = 256
TILES_DEV = 2
CB = 320
HEADS = 8
TOK_DEV = 512
TOKENS = 4096
NT = 16
WIN = 5
NB = 16
N_FRAME = 8
N_HEAD = 4


def drawn_pair(key):
    folded = jax.random.fold_in(key, 71)
    shape = (TOKENS, HEADS * HD)
    query_part = jnp.clip(jax.random.normal(jax.random.fold_in(folded, 1), shape, jnp.float32), -4.5, 4.5)
    key_part = jnp.clip(jax.random.normal(jax.random.fold_in(folded, 2), shape, jnp.float32), -4.5, 4.5)
    return (query_part, key_part)


def draw_query_states(key, part):
    return drawn_pair(key)[0].astype(jnp.bfloat16)


def draw_key_states(key, part):
    return drawn_pair(key)[1].astype(jnp.bfloat16)


def draw_upstream(key, part):
    row_index = jnp.arange(TOKENS, dtype=jnp.float32)
    rising = 1.0 + 2.0 * row_index / max(TOKENS - 1, 1)
    row_scale = rising * jnp.exp(jax.random.uniform(jax.random.fold_in(key, 11), (TOKENS,), jnp.float32, 0.0, math.log(3.0)))
    col_scale = 0.2 * jnp.exp(jax.random.uniform(jax.random.fold_in(key, 12), (D,), jnp.float32, 0.0, math.log(10.0)))
    values_drawn = jnp.clip(jax.random.normal(jax.random.fold_in(key, 13), (TOKENS, D), jnp.float32), -4.0, 4.0)
    return (values_drawn * row_scale[:, None] * col_scale[None, :]).astype(jnp.bfloat16)


def draw_tile_mask(key, part):
    random_bits = jax.random.randint(jax.random.fold_in(key, 21), (NT, WIN), 0, 2, dtype=jnp.int32)
    columns = jnp.arange(WIN, dtype=jnp.int32)[None, :]
    return jnp.where(columns == TILES_DEV, 1, random_bits).astype(jnp.int32)


def shard_levels(key, extent, split, least, largest):
    def one(position, shards_of):
        heights = jax.random.uniform(jax.random.fold_in(jax.random.fold_in(key, 6), position), (shards_of,), jnp.float32, least / len(split), largest / len(split))
        return jnp.repeat(jnp.exp(heights), extent[position] // shards_of).reshape((-1,) + (1,) * (len(extent) - position - 1))

    level = one(*split[0])
    for cut in split[1:]:
        level = level * one(*cut)
    return level


def normal_values(own_key, dims, deviation, bound, cuts=(), held_as=jnp.bfloat16):
    factor_of = shard_levels(own_key, dims, cuts, -0.22, 0.18) if cuts else 1.0
    entries = jax.random.normal(own_key, dims, jnp.float32) * deviation * factor_of
    return jnp.minimum(jnp.maximum(entries, -bound), bound).astype(held_as)


def setup_inputs(seed: int = 0) -> dict:
    splits = jax.random.split(jax.random.key(seed), 7)
    return {
        "query_states": draw_query_states(jax.random.fold_in(splits[6], 71), 0),
        "key_states": draw_key_states(jax.random.fold_in(splits[6], 71), 0),
        "value_states": normal_values(splits[2], (TOKENS, HEADS * HD), 4.0, 24.0, ((0, 8), (1, 4))),
        "out_weight": normal_values(splits[3], (HEADS * HD, D), (HEAD_DEV * HD * 4) ** -0.5, 0.1875, ((0, 4),)),
        "upstream": draw_upstream(jax.random.fold_in(splits[6], 71), 0),
        "tile_mask": draw_tile_mask(jax.random.fold_in(splits[6], 71), 0),
    }


epsilon = 1e-06

def tile_allowed(tile_mask, query_tiles, key_tiles):
    tile_count = tile_mask.shape[0]
    window = tile_mask.shape[1]
    reach_tiles = (window - 1) // 2
    row_hits = (query_tiles[:, None] == jnp.arange(tile_count, dtype=jnp.int32)[None, :]).astype(jnp.int32)
    picked = lax.optimization_barrier(jnp.sum(row_hits[:, :, None] * tile_mask[None, :, :], axis=1))
    offsets = key_tiles[None, :] - query_tiles[:, None] + reach_tiles
    col_hits = offsets[:, :, None] == jnp.arange(window, dtype=jnp.int32)[None, None, :]
    chosen = lax.optimization_barrier(jnp.sum(jnp.where(col_hits, picked[:, None, :], 0), axis=2))
    query_inside = (query_tiles >= 0) & (query_tiles < tile_count)
    key_inside = (key_tiles >= 0) & (key_tiles < tile_count)
    return (chosen > 0) & query_inside[:, None] & key_inside[None, :]

def masked_scores(queries, key_rows, query_tile, key_tile, tile_mask):
    scaling = 1.0 / math.sqrt(queries.shape[2])
    scores = jnp.einsum('thd,shd->hts', queries.astype(jnp.float32), key_rows.astype(jnp.float32)) * scaling
    heads_here = scores.shape[0]
    query_count = queries.shape[0] // TILE
    key_count = key_rows.shape[0] // TILE
    allowed = tile_allowed(tile_mask, query_tile + jnp.arange(query_count, dtype=jnp.int32), key_tile + jnp.arange(key_count, dtype=jnp.int32))
    blocked = scores.reshape(heads_here, query_count, TILE, key_count, TILE)
    blocked = jnp.where(allowed[None, :, None, :, None], blocked, jnp.float32(-1e+30))
    return blocked.reshape(scores.shape)

def log_total(scores):
    peak = lax.optimization_barrier(jnp.max(scores, axis=2))
    return peak + jnp.log(lax.optimization_barrier(jnp.sum(jnp.exp(scores - peak[:, :, None]), axis=2)))

def reference(query_states, key_states, value_states, out_weight, upstream, tile_mask):
    scaling = 1.0 / math.sqrt(HD)
    queries = query_states.reshape(TOKENS, HEADS, HD)
    key_all = key_states.reshape(TOKENS, HEADS, HD)
    value_all = value_states.reshape(TOKENS, HEADS, HD)
    padding = jnp.zeros((TOK_DEV, HEADS, HD), jnp.bfloat16)
    keys_pad = jnp.concatenate([padding, key_all, padding], axis=0)
    values_pad = jnp.concatenate([padding, value_all, padding], axis=0)
    block_ids = jnp.arange(N_FRAME, dtype=jnp.int32)

    def forward_block(block_id):
        first_row = (block_id * TOK_DEV).astype(jnp.int32)
        query_rows = lax.dynamic_slice_in_dim(queries, first_row, TOK_DEV, 0)
        key_rows = lax.dynamic_slice_in_dim(keys_pad, first_row, 3 * TOK_DEV, 0)
        value_rows = lax.dynamic_slice_in_dim(values_pad, first_row, 3 * TOK_DEV, 0)
        scores = masked_scores(query_rows, key_rows, block_id * TILES_DEV, block_id * TILES_DEV - TILES_DEV, tile_mask)
        totals = log_total(scores)
        weights = jnp.exp(scores - totals[:, :, None]).astype(jnp.bfloat16)
        output = jnp.einsum('hts,shd->thd', weights.astype(jnp.float32), value_rows.astype(jnp.float32))
        return (output.astype(jnp.bfloat16), totals)
    outputs, totals_blocks = lax.map(forward_block, block_ids)
    attended3 = outputs.reshape(TOKENS, HEADS, HD)
    attended = attended3.reshape(TOKENS, HEADS * HD)
    totals_all = jnp.transpose(totals_blocks, (1, 0, 2)).reshape(HEADS, TOKENS)
    group_width = HEAD_DEV * HD

    def add_group(group_id, running):
        first_col = (group_id * group_width).astype(jnp.int32)
        group_cols = lax.dynamic_slice_in_dim(attended, first_col, group_width, 1)
        group_rows = lax.dynamic_slice_in_dim(out_weight, first_col, group_width, 0)
        group_sum = jnp.dot(group_cols, group_rows, preferred_element_type=jnp.float32).astype(jnp.bfloat16)
        group_sum = lax.optimization_barrier(group_sum)
        return running + group_sum.astype(jnp.float32)
    projected = lax.fori_loop(0, N_HEAD, add_group, jnp.zeros((TOKENS, D), jnp.float32)).astype(jnp.bfloat16)
    grad_attended = lax.dot_general(upstream, out_weight, (((1,), (1,)), ((), ())), preferred_element_type=jnp.float32).astype(jnp.bfloat16)
    grads3 = grad_attended.reshape(TOKENS, HEADS, HD)
    deltas = lax.optimization_barrier(jnp.sum(grads3.astype(jnp.float32) * attended3.astype(jnp.float32), axis=2)).T

    def query_block(block_id):
        first_row = (block_id * TOK_DEV).astype(jnp.int32)
        query_rows = lax.dynamic_slice_in_dim(queries, first_row, TOK_DEV, 0)
        grad_rows = lax.dynamic_slice_in_dim(grads3, first_row, TOK_DEV, 0)
        key_rows = lax.dynamic_slice_in_dim(keys_pad, first_row, 3 * TOK_DEV, 0)
        value_rows = lax.dynamic_slice_in_dim(values_pad, first_row, 3 * TOK_DEV, 0)
        total_rows = lax.dynamic_slice_in_dim(totals_all, first_row, TOK_DEV, 1)
        delta_rows = lax.dynamic_slice_in_dim(deltas, first_row, TOK_DEV, 1)
        scores = masked_scores(query_rows, key_rows, block_id * TILES_DEV, block_id * TILES_DEV - TILES_DEV, tile_mask)
        attention = jnp.exp(scores - total_rows[:, :, None])
        grad_probs = jnp.einsum('thd,shd->hts', grad_rows.astype(jnp.float32), value_rows.astype(jnp.float32))
        grad_scores = (attention * (grad_probs - delta_rows[:, :, None])).astype(jnp.bfloat16)
        result = jnp.einsum('hts,shd->thd', grad_scores.astype(jnp.float32), key_rows.astype(jnp.float32)) * scaling
        return result.astype(jnp.bfloat16)
    grad_query = lax.map(query_block, block_ids).reshape(TOKENS, HEADS * HD)
    queries_pad = jnp.concatenate([padding, queries, padding], axis=0)
    grads_pad = jnp.concatenate([padding, grads3, padding], axis=0)
    stat_pad = jnp.zeros((HEADS, TOK_DEV), jnp.float32)
    totals_pad = jnp.concatenate([stat_pad, totals_all, stat_pad], axis=1)
    deltas_pad = jnp.concatenate([stat_pad, deltas, stat_pad], axis=1)

    def key_block(block_id):
        first_row = (block_id * TOK_DEV).astype(jnp.int32)
        query_rows = lax.dynamic_slice_in_dim(queries_pad, first_row, 3 * TOK_DEV, 0)
        grad_rows = lax.dynamic_slice_in_dim(grads_pad, first_row, 3 * TOK_DEV, 0)
        total_rows = lax.dynamic_slice_in_dim(totals_pad, first_row, 3 * TOK_DEV, 1)
        delta_rows = lax.dynamic_slice_in_dim(deltas_pad, first_row, 3 * TOK_DEV, 1)
        key_rows = lax.dynamic_slice_in_dim(key_all, first_row, TOK_DEV, 0)
        value_rows = lax.dynamic_slice_in_dim(value_all, first_row, TOK_DEV, 0)
        scores = masked_scores(query_rows, key_rows, block_id * TILES_DEV - TILES_DEV, block_id * TILES_DEV, tile_mask)
        attention = jnp.exp(scores - total_rows[:, :, None])
        weights = attention.astype(jnp.bfloat16)
        grad_probs = jnp.einsum('thd,shd->hts', grad_rows.astype(jnp.float32), value_rows.astype(jnp.float32))
        grad_scores = (attention * (grad_probs - delta_rows[:, :, None])).astype(jnp.bfloat16)
        grad_keys = jnp.einsum('hts,thd->shd', grad_scores.astype(jnp.float32), query_rows.astype(jnp.float32)) * scaling
        grad_values = jnp.einsum('hts,thd->shd', weights.astype(jnp.float32), grad_rows.astype(jnp.float32))
        return (grad_keys.astype(jnp.bfloat16), grad_values.astype(jnp.bfloat16))
    grad_keys, grad_values = lax.map(key_block, block_ids)
    grad_key = grad_keys.reshape(TOKENS, HEADS * HD)
    grad_value = grad_values.reshape(TOKENS, HEADS * HD)
    weight_grad = lax.dot_general(attended, upstream, (((0,), (0,)), ((), ())), preferred_element_type=jnp.float32)
    blocks = weight_grad.reshape(HEADS, HD, NB, CB)
    highest = lax.Precision.HIGHEST
    traces = jnp.einsum('hebc,hebc->hb', blocks, blocks, precision=highest)
    divisor = (traces + epsilon)[:, :, None, None]
    gram_left = HD * jnp.einsum('hebc,hfbc->hbef', blocks, blocks, precision=highest) / divisor
    gram_right = CB * jnp.einsum('hebc,hebd->hbcd', blocks, blocks, precision=highest) / divisor
    return (attended, projected, grad_query, grad_key, grad_value, gram_left, gram_right)
```

```python
import functools
import math

import jax
import jax.numpy as jnp
from jax import lax
from jax.experimental import pallas as pl
from jax.experimental.pallas import tpu as pltpu
from jax.sharding import PartitionSpec as P

HD = 128
TILE = 256
CB = 320

epsilon = 1e-06
F32 = jnp.float32
BF16 = jnp.bfloat16
MESH = pl.DeviceIdType.MESH
NT = (((1,), (1,)), ((), ()))


def dot(a, b):
    return jnp.dot(a, b, preferred_element_type=F32)


def dot_nt(a, b):
    return lax.dot_general(a, b, NT, preferred_element_type=F32)


def kernel(
    nf, nh, tiles_all,
    q_hbm, k_hbm, v_hbm, w_hbm, wc_hbm, up_hbm, tm_ref,
    att_o, proj_o, dq_o, dk_o, dv_o, gl_o, gr_o,
    qv, kext, vext, wv, upb, wcols, attall, wts, attT, ga, gaT,
    kT, vT, dkacc, dvacc, ghs, ghr, outs, projv, pa, sa, pb, sb, rb,
    load_sem, up_sem, halo_s, halo_r, w_s, w_r, fw_s, fw_r, at_s, at_r,
    sa_s, sa_r, rb_s, rb_r, gh_s, gh_r, out_sem,
):
    f = lax.axis_index("frame")
    hd = lax.axis_index("head")
    core = lax.rem(f, 2)
    chip = lax.div(f, 2)
    chips = nf // 2
    sib = f + 1 - 2 * core
    tok, hw = qv.shape
    heads = hw // HD
    qt = tok // TILE
    win = tm_ref.shape[1]
    reach = (win - 1) // 2
    halo = reach * TILE
    span = win * TILE
    half = hw // 2
    cols = wcols.shape[2]
    cb = upb.shape[2]
    scale = 1.0 / math.sqrt(HD)

    barrier = pltpu.get_barrier_semaphore()
    for d in range(1, nf):
        pl.semaphore_signal(barrier, inc=1, device_id=(lax.rem(f + d, nf), hd), device_id_type=MESH)
    for d in range(1, nh):
        pl.semaphore_signal(barrier, inc=1, device_id=(f, lax.rem(hd + d, nh)), device_id_type=MESH)

    def w_block(j, rows):
        if cols % 128 == 0:
            return w_hbm.at[rows, pl.ds(pl.multiple_of(j * cols, 128), cols)]
        return wc_hbm.at[j, rows]

    def up_block(j):
        if cb % 128 == 0:
            return up_hbm.at[:, pl.ds(j * cb, cb)]
        return up_hbm.at[j]

    center = pl.ds(halo, tok)
    loads = [
        pltpu.make_async_copy(w_hbm, wv, load_sem.at[0]),
        pltpu.make_async_copy(k_hbm, kext.at[center], load_sem.at[1]),
        pltpu.make_async_copy(v_hbm, vext.at[center], load_sem.at[2]),
        pltpu.make_async_copy(q_hbm, qv, load_sem.at[3]),
        pltpu.make_async_copy(w_block(hd, pl.ds(0, hw)), wcols.at[hd], load_sem.at[4]),
    ]
    ups = [pltpu.make_async_copy(up_block(j), upb.at[j], up_sem.at[j]) for j in range(nf)]
    loads[0].start()
    for cp in ups:
        cp.start()
    for cp in loads[1:]:
        cp.start()

    pl.semaphore_wait(barrier, nf + nh - 2)

    def halo_copy(side, which):
        src = (k_hbm, v_hbm)[which]
        dst = (kext, vext)[which]
        rows = pl.ds(0, halo) if side == 0 else pl.ds(halo + tok, halo)
        part = pl.ds(tok - halo, halo) if side == 0 else pl.ds(0, halo)
        to = f + 1 if side == 0 else f - 1
        return pltpu.make_async_remote_copy(
            src_ref=src.at[part], dst_ref=dst.at[rows],
            send_sem=halo_s.at[side, which], recv_sem=halo_r.at[side, which],
            device_id=(to, hd), device_id_type=MESH)

    has_next = f < nf - 1
    has_prev = f > 0

    @pl.when(has_next)
    def _():
        for which in range(2):
            halo_copy(0, which).start()

    @pl.when(has_prev)
    def _():
        for which in range(2):
            halo_copy(1, which).start()

    my_rows = pl.ds(pl.multiple_of(core * half, half), half)
    w_copies = []
    for d in range(1, nh):
        j = lax.rem(hd + d, nh)
        cp = pltpu.make_async_remote_copy(
            src_ref=w_block(j, my_rows), dst_ref=wcols.at[hd, my_rows],
            send_sem=w_s.at[d], recv_sem=w_r.at[d],
            device_id=(f, j), device_id_type=MESH)
        cp.start()
        w_copies.append(cp)

    @pl.when(jnp.logical_not(has_prev))
    def _():
        kext[pl.ds(0, halo)] = jnp.zeros((halo, hw), BF16)
        vext[pl.ds(0, halo)] = jnp.zeros((halo, hw), BF16)

    @pl.when(jnp.logical_not(has_next))
    def _():
        kext[pl.ds(halo + tok, halo)] = jnp.zeros((halo, hw), BF16)
        vext[pl.ds(halo + tok, halo)] = jnp.zeros((halo, hw), BF16)

    loads[0].wait()
    acc = None
    for j in range(nf):
        ups[j].wait()
        part = dot_nt(wv[:, j * cb:(j + 1) * cb], upb[j])
        acc = part if acc is None else acc + part
    gaT[...] = acc.astype(BF16)
    ga[...] = acc.T.astype(BF16)
    for cp in loads[1:]:
        cp.wait()

    @pl.when(has_prev)
    def _():
        for which in range(2):
            halo_copy(0, which).wait_recv()

    @pl.when(has_next)
    def _():
        for which in range(2):
            halo_copy(1, which).wait_recv()

    kT[...] = kext[...].T
    vT[...] = vext[...].T

    def hcols(h):
        return pl.ds(h * HD, HD)

    for h in range(heads):
        for i in range(qt):
            rows = pl.ds(i * TILE, TILE)
            keys = pl.ds(i * TILE, span)
            s = dot_nt(kext[keys, hcols(h)], qv[rows, hcols(h)])
            parts = []
            tile = f * qt + i
            for o in range(win):
                b = tile + o - reach
                inside = jnp.where(jnp.logical_and(b >= 0, b < tiles_all), 1.0, 0.0)
                m = tm_ref[tile, o].astype(F32) * inside
                parts.append(s[o * TILE:(o + 1) * TILE] * (m * scale) + (m * 1e30 - 1e30))
            s = jnp.concatenate(parts, axis=0)
            p = jnp.exp(s - jnp.max(s, axis=0, keepdims=True))
            total = jnp.sum(p, axis=0, keepdims=True)
            wt = (p * (1.0 / total)).astype(BF16)
            wts[h * qt + i] = wt
            attT[hcols(h), rows] = dot(vT[hcols(h), keys], wt).astype(BF16)
    attall[hd] = attT[...].T

    att_out = pltpu.make_async_copy(attall.at[hd], att_o, out_sem.at[0])
    att_out.start()
    at_copies = []
    for d in range(1, nh):
        cp = pltpu.make_async_remote_copy(
            src_ref=attall.at[hd], dst_ref=attall.at[hd],
            send_sem=at_s.at[d], recv_sem=at_r.at[d],
            device_id=(f, lax.rem(hd + d, nh)), device_id_type=MESH)
        cp.start()
        at_copies.append(cp)

    order = [*range(1, chips), 0]
    sa_copies = {}
    for d in order:
        q = lax.rem(chip + d, chips)
        pa[d] = dot(attT[...], upb[2 * q + 1 - core]).astype(BF16)
        cp = pltpu.make_async_remote_copy(
            src_ref=pa.at[d], dst_ref=sa.at[d], send_sem=sa_s.at[d], recv_sem=sa_r.at[d],
            device_id=(sib, hd), device_id_type=MESH)
        cp.start()
        sa_copies[d] = cp
    rb_copies = {}
    for d in order:
        q = lax.rem(chip + d, chips)
        part = dot(attT[...], upb[2 * q + core])
        sa_copies[d].wait_recv()
        part = part + sa[d].astype(F32)
        if d == 0:
            pb[...] = part
        else:
            sb[d] = part.astype(BF16)
            cp = pltpu.make_async_remote_copy(
                src_ref=sb.at[d], dst_ref=rb.at[d], send_sem=rb_s.at[d], recv_sem=rb_r.at[d],
                device_id=(2 * q + core, hd), device_id_type=MESH)
            cp.start()
            rb_copies[d] = cp

    dkacc[...] = jnp.zeros_like(dkacc)
    dvacc[...] = jnp.zeros_like(dvacc)
    for h in range(heads):
        for i in range(qt):
            rows = pl.ds(i * TILE, TILE)
            keys = pl.ds(i * TILE, span)
            wt = wts[h * qt + i]
            g = dot_nt(vext[keys, hcols(h)], ga[rows, hcols(h)])
            delta = jnp.sum(
                gaT[hcols(h), rows].astype(F32) * attT[hcols(h), rows].astype(F32),
                axis=0, keepdims=True)
            ds = (wt.astype(F32) * (g - delta)).astype(BF16)
            dqT = dot(kT[hcols(h), keys], ds) * scale
            outs[0, rows, hcols(h)] = dqT.T.astype(BF16)
            dkacc[keys, hcols(h)] += dot(ds, qv[rows, hcols(h)])
            dvacc[keys, hcols(h)] += dot(wt, ga[rows, hcols(h)])

    dq_out = pltpu.make_async_copy(outs.at[0], dq_o, out_sem.at[1])
    dq_out.start()

    def gh_copy(side):
        to = f + 1 if side == 0 else f - 1
        return pltpu.make_async_remote_copy(
            src_ref=ghs.at[side], dst_ref=ghr.at[side],
            send_sem=gh_s.at[side], recv_sem=gh_r.at[side],
            device_id=(to, hd), device_id_type=MESH)

    upper = pl.ds(halo + tok, halo)
    lower = pl.ds(0, halo)
    ghs[0, 0] = (dkacc[upper] * scale).astype(BF16)
    ghs[0, 1] = dvacc[upper].astype(BF16)
    ghs[1, 0] = (dkacc[lower] * scale).astype(BF16)
    ghs[1, 1] = dvacc[lower].astype(BF16)

    @pl.when(has_next)
    def _():
        gh_copy(0).start()

    @pl.when(has_prev)
    def _():
        gh_copy(1).start()

    @pl.when(jnp.logical_not(has_prev))
    def _():
        ghr[0] = jnp.zeros(ghr.shape[1:], BF16)

    @pl.when(jnp.logical_not(has_next))
    def _():
        ghr[1] = jnp.zeros(ghr.shape[1:], BF16)

    fw_copies = []
    for d in range(1, nh):
        w_copies[d - 1].wait_recv()
        s = lax.rem(hd + nh - d, nh)
        cp = pltpu.make_async_remote_copy(
            src_ref=wcols.at[s, my_rows], dst_ref=wcols.at[s, my_rows],
            send_sem=fw_s.at[d], recv_sem=fw_r.at[d],
            device_id=(sib, hd), device_id_type=MESH)
        cp.start()
        fw_copies.append(cp)

    @pl.when(has_prev)
    def _():
        gh_copy(0).wait_recv()

    @pl.when(has_next)
    def _():
        gh_copy(1).wait_recv()

    first, last = slice(0, halo), slice(tok - halo, tok)
    for which, (full, factor) in enumerate(((dkacc, scale), (dvacc, 1.0))):
        full[pl.ds(halo, halo)] += ghr[0, which].astype(F32) * (1.0 / factor)
        full[pl.ds(tok, halo)] += ghr[1, which].astype(F32) * (1.0 / factor)
        outs[1 + which] = (full[center] * factor).astype(BF16)
    dk_out = pltpu.make_async_copy(outs.at[1], dk_o, out_sem.at[2])
    dv_out = pltpu.make_async_copy(outs.at[2], dv_o, out_sem.at[3])
    dk_out.start()
    dv_out.start()

    grad = pb[...]
    for d in range(1, chips):
        rb_copies[d].wait_recv()
        grad = grad + rb[d].astype(F32)
    for h in range(heads):
        for n in range(cb // CB):
            block = grad[h * HD:(h + 1) * HD, n * CB:(n + 1) * CB]
            trace = jnp.sum(jnp.sum(block * block, axis=0, keepdims=True), axis=1, keepdims=True)
            inverse = 1.0 / (trace + epsilon)
            small = block.astype(BF16)
            gl_o[h, n] = dot_nt(small, small) * (inverse * HD)
            gr_o[h, n] = dot(block.T.astype(BF16), small) * (inverse * CB)

    at_copies_all = at_copies
    acc = dot(attall[hd], wcols[hd])
    for d in range(1, nh):
        s = lax.rem(hd + nh - d, nh)
        at_copies_all[d - 1].wait_recv()
        fw_copies[d - 1].wait_recv()
        acc = acc + dot(attall[s], wcols[s])
    projv[...] = acc.astype(BF16)
    proj_out = pltpu.make_async_copy(projv, proj_o, out_sem.at[4])
    proj_out.start()

    for cp in (*w_copies, *fw_copies, *at_copies, *sa_copies.values(), *rb_copies.values()):
        cp.wait_send()

    @pl.when(has_next)
    def _():
        for which in range(2):
            halo_copy(0, which).wait_send()
        gh_copy(0).wait_send()

    @pl.when(has_prev)
    def _():
        for which in range(2):
            halo_copy(1, which).wait_send()
        gh_copy(1).wait_send()

    for cp in (att_out, dq_out, dk_out, dv_out, proj_out):
        cp.wait()


def local(query_states, key_states, value_states, out_weight, upstream, tile_mask):
    nf = lax.axis_size("frame")
    nh = lax.axis_size("head")
    tok, hw = query_states.shape
    heads = hw // HD
    width = out_weight.shape[1]
    cols = width // nh
    cb = width // nf
    chips = nf // 2
    win = tile_mask.shape[1]
    reach = (win - 1) // 2
    halo = reach * TILE
    ext = tok + 2 * halo
    w_in = out_weight
    if cols % 128:
        w_in = out_weight.reshape(hw, nh, cols).transpose(1, 0, 2)
    up_in = upstream
    if cb % 128:
        up_in = upstream.reshape(tok, nf, cb).transpose(1, 0, 2)
    anywhere = pl.BlockSpec(memory_space=pl.ANY)
    vmem = pl.BlockSpec(memory_space=pltpu.VMEM)
    dma = pltpu.SemaphoreType.DMA
    return pl.pallas_call(
        functools.partial(kernel, nf, nh, tile_mask.shape[0]),
        out_shape=(
            jax.ShapeDtypeStruct((tok, hw), BF16),
            jax.ShapeDtypeStruct((tok, cols), BF16),
            jax.ShapeDtypeStruct((tok, hw), BF16),
            jax.ShapeDtypeStruct((tok, hw), BF16),
            jax.ShapeDtypeStruct((tok, hw), BF16),
            jax.ShapeDtypeStruct((heads, cb // CB, HD, HD), F32),
            jax.ShapeDtypeStruct((heads, cb // CB, CB, CB), F32),
        ),
        in_specs=[anywhere] * 6 + [pl.BlockSpec(memory_space=pltpu.SMEM)],
        out_specs=(anywhere,) * 5 + (vmem, vmem),
        scratch_shapes=[
            pltpu.VMEM((tok, hw), BF16),
            pltpu.VMEM((ext, hw), BF16),
            pltpu.VMEM((ext, hw), BF16),
            pltpu.VMEM((hw, width), BF16),
            pltpu.VMEM((nf, tok, cb), BF16),
            pltpu.VMEM((nh, hw, cols), BF16),
            pltpu.VMEM((nh, tok, hw), BF16),
            pltpu.VMEM((heads * (tok // TILE), win * TILE, TILE), BF16),
            pltpu.VMEM((hw, tok), BF16),
            pltpu.VMEM((tok, hw), BF16),
            pltpu.VMEM((hw, tok), BF16),
            pltpu.VMEM((hw, ext), BF16),
            pltpu.VMEM((hw, ext), BF16),
            pltpu.VMEM((ext, hw), F32),
            pltpu.VMEM((ext, hw), F32),
            pltpu.VMEM((2, 2, halo, hw), BF16),
            pltpu.VMEM((2, 2, halo, hw), BF16),
            pltpu.VMEM((3, tok, hw), BF16),
            pltpu.VMEM((tok, cols), BF16),
            pltpu.VMEM((chips, hw, cb), BF16),
            pltpu.VMEM((chips, hw, cb), BF16),
            pltpu.VMEM((hw, cb), F32),
            pltpu.VMEM((chips, hw, cb), BF16),
            pltpu.VMEM((chips, hw, cb), BF16),
            dma((5,)),
            dma((nf,)),
            dma((2, 2)), dma((2, 2)),
            dma((nh,)), dma((nh,)),
            dma((nh,)), dma((nh,)),
            dma((nh,)), dma((nh,)),
            dma((chips,)), dma((chips,)),
            dma((chips,)), dma((chips,)),
            dma((2,)), dma((2,)),
            dma((5,)),
        ],
        compiler_params=pltpu.CompilerParams(
            collective_id=0, has_side_effects=True, vmem_limit_bytes=56 * 1024 * 1024),
    )(query_states, key_states, value_states, out_weight, w_in, up_in, tile_mask)


def solution(mesh):
    return jax.shard_map(
        local,
        mesh=mesh,
        in_specs=(
            P("frame", "head"),
            P("frame", "head"),
            P("frame", "head"),
            P("head", None),
            P("frame", None),
            P(),
        ),
        out_specs=(
            P("frame", "head"),
            P("frame", "head"),
            P("frame", "head"),
            P("frame", "head"),
            P("frame", "head"),
            P("head", "frame", None, None),
            P("head", "frame", None, None),
        ),
        check_vma=False,
    )
```

```python
import functools
import math

import jax
import jax.numpy as jnp
from jax import lax
from jax.experimental import pallas as pl
from jax.experimental.pallas import tpu as pltpu
from jax.sharding import PartitionSpec as P

HD = 128
TILE = 256
CB = 320

epsilon = 1e-06
F32 = jnp.float32
BF16 = jnp.bfloat16
MESH = pl.DeviceIdType.MESH
NT = (((1,), (1,)), ((), ()))


def dot(a, b):
    return jnp.dot(a, b, preferred_element_type=F32)


def dot_nt(a, b):
    return lax.dot_general(a, b, NT, preferred_element_type=F32)


def kernel(
    nf, nh, tiles_all,
    q_hbm, k_hbm, v_hbm, w_hbm, wc_hbm, up_hbm, tm_ref,
    att_o, proj_o, dq_o, dk_o, dv_o, grad_o,
    qv, kext, vext, wv, upb, wcols, attall, wts, attT, ga, gaT,
    kT, vT, dkacc, dvacc, ghs, ghr, outs, projv, pa, sa, pb, sb, rb,
    load_sem, up_sem, halo_s, halo_r, w_s, w_r, tw_s, tw_r, fw_s, fw_r, at_s, at_r,
    sa_s, sa_r, rb_s, rb_r, gh_s, gh_r, out_sem,
):
    f = lax.axis_index("frame")
    hd = lax.axis_index("head")
    core = lax.rem(f, 2)
    chip = lax.div(f, 2)
    chips = nf // 2
    sib = f + 1 - 2 * core
    tok, hw = qv.shape
    heads = hw // HD
    qt = tok // TILE
    win = tm_ref.shape[0]
    reach = (win - 1) // 2
    halo = reach * TILE
    span = win * TILE
    half = hw // 2
    cols = wcols.shape[2]
    cb = upb.shape[2]
    scale = 1.0 / math.sqrt(HD)

    barrier = pltpu.get_barrier_semaphore()
    for d in range(1, nf):
        pl.semaphore_signal(barrier, inc=1, device_id=(lax.rem(f + d, nf), hd), device_id_type=MESH)
    for d in range(1, nh):
        pl.semaphore_signal(barrier, inc=1, device_id=(f, lax.rem(hd + d, nh)), device_id_type=MESH)

    def w_block(j, rows):
        if cols % 128 == 0:
            return w_hbm.at[rows, pl.ds(pl.multiple_of(j * cols, 128), cols)]
        return wc_hbm.at[j, rows]

    def up_block(j):
        if cb % 128 == 0:
            return up_hbm.at[:, pl.ds(j * cb, cb)]
        return up_hbm.at[j]

    center = pl.ds(halo, tok)
    loads = [
        pltpu.make_async_copy(w_hbm, wv, load_sem.at[0]),
        pltpu.make_async_copy(k_hbm, kext.at[center], load_sem.at[1]),
        pltpu.make_async_copy(v_hbm, vext.at[center], load_sem.at[2]),
        pltpu.make_async_copy(q_hbm, qv, load_sem.at[3]),
        pltpu.make_async_copy(w_block(hd, pl.ds(0, hw)), wcols.at[hd], load_sem.at[4]),
    ]
    ups = [pltpu.make_async_copy(up_block(j), upb.at[j], up_sem.at[j]) for j in range(nf)]
    loads[0].start()
    for cp in ups:
        cp.start()
    for cp in loads[1:]:
        cp.start()

    pl.semaphore_wait(barrier, nf + nh - 2)

    def halo_copy(side, which):
        src = (k_hbm, v_hbm)[which]
        dst = (kext, vext)[which]
        rows = pl.ds(0, halo) if side == 0 else pl.ds(halo + tok, halo)
        part = pl.ds(tok - halo, halo) if side == 0 else pl.ds(0, halo)
        to = f + 1 if side == 0 else f - 1
        return pltpu.make_async_remote_copy(
            src_ref=src.at[part], dst_ref=dst.at[rows],
            send_sem=halo_s.at[side, which], recv_sem=halo_r.at[side, which],
            device_id=(to, hd), device_id_type=MESH)

    has_next = f < nf - 1
    has_prev = f > 0

    for which in range(2):
        @pl.when(has_next)
        def _():
            halo_copy(0, which).start()

        @pl.when(has_prev)
        def _():
            halo_copy(1, which).start()

    my_rows = pl.ds(pl.multiple_of(core * half, half), half)
    quarter = half // 2
    upper_half = lax.div(f, nf // 2)
    other = lax.rem(f + nf // 2, nf)
    my_part = pl.ds(pl.multiple_of(core * half + upper_half * quarter, quarter), quarter)
    w_copies = []
    for d in range(1, nh):
        j = lax.rem(hd + d, nh)
        cp = pltpu.make_async_remote_copy(
            src_ref=w_block(j, my_part), dst_ref=wcols.at[hd, my_part],
            send_sem=w_s.at[d], recv_sem=w_r.at[d],
            device_id=(f, j), device_id_type=MESH)
        cp.start()
        w_copies.append(cp)

    @pl.when(jnp.logical_not(has_prev))
    def _():
        kext[pl.ds(0, halo)] = jnp.zeros((halo, hw), BF16)
        vext[pl.ds(0, halo)] = jnp.zeros((halo, hw), BF16)

    @pl.when(jnp.logical_not(has_next))
    def _():
        kext[pl.ds(halo + tok, halo)] = jnp.zeros((halo, hw), BF16)
        vext[pl.ds(halo + tok, halo)] = jnp.zeros((halo, hw), BF16)

    loads[0].wait()
    acc = None
    for j in range(nf):
        ups[j].wait()
        part = dot_nt(wv[:, j * cb:(j + 1) * cb], upb[j])
        acc = part if acc is None else acc + part
    gaT[...] = acc.astype(BF16)
    ga[...] = acc.T.astype(BF16)
    for cp in loads[1:]:
        cp.wait()

    def halo_arrived(which):
        @pl.when(has_prev)
        def _():
            halo_copy(0, which).wait_recv()

        @pl.when(has_next)
        def _():
            halo_copy(1, which).wait_recv()

    halo_arrived(0)

    def hcols(h):
        return pl.ds(h * HD, HD)

    for h in range(heads):
        for i in range(qt):
            rows = pl.ds(i * TILE, TILE)
            keys = pl.ds(i * TILE, span)
            s = dot_nt(kext[keys, hcols(h)], qv[rows, hcols(h)])
            parts = []
            tile = f * qt + i
            for o in range(win):
                b = tile + o - reach
                inside = jnp.where(jnp.logical_and(b >= 0, b < tiles_all), 1.0, 0.0)
                m = tm_ref[o, tile].astype(F32) * inside
                parts.append(s[o * TILE:(o + 1) * TILE] * (m * scale) + (m * 1e30 - 1e30))
            s = jnp.concatenate(parts, axis=0)
            p = jnp.exp(s - jnp.max(s, axis=0, keepdims=True))
            total = jnp.sum(p, axis=0, keepdims=True)
            wt = (p * (1.0 / total)).astype(BF16)
            wts[h * qt + i] = wt
    kT[...] = kext[...].T
    halo_arrived(1)
    vT[...] = vext[...].T
    for h in range(heads):
        for i in range(qt):
            rows = pl.ds(i * TILE, TILE)
            keys = pl.ds(i * TILE, span)
            attT[hcols(h), rows] = dot(vT[hcols(h), keys], wts[h * qt + i]).astype(BF16)
    attall[hd] = attT[...].T

    att_out = pltpu.make_async_copy(attall.at[hd], att_o, out_sem.at[0])
    att_out.start()
    at_copies = []
    for d in range(1, nh):
        cp = pltpu.make_async_remote_copy(
            src_ref=attall.at[hd], dst_ref=attall.at[hd],
            send_sem=at_s.at[d], recv_sem=at_r.at[d],
            device_id=(f, lax.rem(hd + d, nh)), device_id_type=MESH)
        cp.start()
        at_copies.append(cp)

    tw_copies = []
    for d in range(1, nh):
        w_copies[d - 1].wait_recv()
        s = lax.rem(hd + nh - d, nh)
        cp = pltpu.make_async_remote_copy(
            src_ref=wcols.at[s, my_part], dst_ref=wcols.at[s, my_part],
            send_sem=tw_s.at[d], recv_sem=tw_r.at[d],
            device_id=(other, hd), device_id_type=MESH)
        cp.start()
        tw_copies.append(cp)

    order = [*range(1, chips), 0]
    sa_copies = {}
    for d in order:
        q = lax.rem(chip + d, chips)
        pa[d] = dot(attT[...], upb[2 * q + 1 - core]).astype(BF16)
        cp = pltpu.make_async_remote_copy(
            src_ref=pa.at[d], dst_ref=sa.at[d], send_sem=sa_s.at[d], recv_sem=sa_r.at[d],
            device_id=(sib, hd), device_id_type=MESH)
        cp.start()
        sa_copies[d] = cp
    rb_copies = {}
    for d in order:
        q = lax.rem(chip + d, chips)
        part = dot(attT[...], upb[2 * q + core])
        sa_copies[d].wait_recv()
        part = part + sa[d].astype(F32)
        if d == 0:
            pb[...] = part
        else:
            sb[d] = part.astype(BF16)
            cp = pltpu.make_async_remote_copy(
                src_ref=sb.at[d], dst_ref=rb.at[d], send_sem=rb_s.at[d], recv_sem=rb_r.at[d],
                device_id=(2 * q + core, hd), device_id_type=MESH)
            cp.start()
            rb_copies[d] = cp

    dkacc[...] = jnp.zeros_like(dkacc)
    dvacc[...] = jnp.zeros_like(dvacc)
    for h in range(heads):
        for i in range(qt):
            rows = pl.ds(i * TILE, TILE)
            keys = pl.ds(i * TILE, span)
            wt = wts[h * qt + i]
            g = dot_nt(vext[keys, hcols(h)], ga[rows, hcols(h)])
            delta = jnp.sum(
                gaT[hcols(h), rows].astype(F32) * attT[hcols(h), rows].astype(F32),
                axis=0, keepdims=True)
            ds = (wt.astype(F32) * (g - delta)).astype(BF16)
            dqT = dot(kT[hcols(h), keys], ds) * scale
            outs[0, rows, hcols(h)] = dqT.T.astype(BF16)
            dkacc[keys, hcols(h)] += dot(ds, qv[rows, hcols(h)])
            dvacc[keys, hcols(h)] += dot(wt, ga[rows, hcols(h)])

    dq_out = pltpu.make_async_copy(outs.at[0], dq_o, out_sem.at[1])
    dq_out.start()

    def gh_copy(side):
        to = f + 1 if side == 0 else f - 1
        return pltpu.make_async_remote_copy(
            src_ref=ghs.at[side], dst_ref=ghr.at[side],
            send_sem=gh_s.at[side], recv_sem=gh_r.at[side],
            device_id=(to, hd), device_id_type=MESH)

    upper = pl.ds(halo + tok, halo)
    lower = pl.ds(0, halo)
    ghs[0, 0] = (dkacc[upper] * scale).astype(BF16)
    ghs[0, 1] = dvacc[upper].astype(BF16)
    ghs[1, 0] = (dkacc[lower] * scale).astype(BF16)
    ghs[1, 1] = dvacc[lower].astype(BF16)

    @pl.when(has_next)
    def _():
        gh_copy(0).start()

    @pl.when(has_prev)
    def _():
        gh_copy(1).start()

    @pl.when(jnp.logical_not(has_prev))
    def _():
        ghr[0] = jnp.zeros(ghr.shape[1:], BF16)

    @pl.when(jnp.logical_not(has_next))
    def _():
        ghr[1] = jnp.zeros(ghr.shape[1:], BF16)

    fw_copies = []
    for d in range(1, nh):
        tw_copies[d - 1].wait_recv()
        s = lax.rem(hd + nh - d, nh)
        cp = pltpu.make_async_remote_copy(
            src_ref=wcols.at[s, my_rows], dst_ref=wcols.at[s, my_rows],
            send_sem=fw_s.at[d], recv_sem=fw_r.at[d],
            device_id=(sib, hd), device_id_type=MESH)
        cp.start()
        fw_copies.append(cp)

    grad = pb[...]
    for d in range(1, chips):
        rb_copies[d].wait_recv()
        grad = grad + rb[d].astype(F32)
    pb[...] = grad
    grad_out = pltpu.make_async_copy(pb, grad_o, out_sem.at[5])
    grad_out.start()

    at_copies_all = at_copies
    acc = dot(attall[hd], wcols[hd])
    for d in range(1, nh):
        s = lax.rem(hd + nh - d, nh)
        at_copies_all[d - 1].wait_recv()
        fw_copies[d - 1].wait_recv()
        acc = acc + dot(attall[s], wcols[s])
    projv[...] = acc.astype(BF16)
    proj_out = pltpu.make_async_copy(projv, proj_o, out_sem.at[4])
    proj_out.start()

    @pl.when(has_prev)
    def _():
        gh_copy(0).wait_recv()

    @pl.when(has_next)
    def _():
        gh_copy(1).wait_recv()

    first, last = slice(0, halo), slice(tok - halo, tok)
    for which, (full, factor) in enumerate(((dkacc, scale), (dvacc, 1.0))):
        full[pl.ds(halo, halo)] += ghr[0, which].astype(F32) * (1.0 / factor)
        full[pl.ds(tok, halo)] += ghr[1, which].astype(F32) * (1.0 / factor)
        outs[1 + which] = (full[center] * factor).astype(BF16)
    dk_out = pltpu.make_async_copy(outs.at[1], dk_o, out_sem.at[2])
    dv_out = pltpu.make_async_copy(outs.at[2], dv_o, out_sem.at[3])
    dk_out.start()
    dv_out.start()

    for cp in (*w_copies, *tw_copies, *fw_copies, *at_copies, *sa_copies.values(), *rb_copies.values()):
        cp.wait_send()

    @pl.when(has_next)
    def _():
        for which in range(2):
            halo_copy(0, which).wait_send()
        gh_copy(0).wait_send()

    @pl.when(has_prev)
    def _():
        for which in range(2):
            halo_copy(1, which).wait_send()
        gh_copy(1).wait_send()

    for cp in (att_out, dq_out, dk_out, dv_out, proj_out, grad_out):
        cp.wait()


def finish(*refs):
    sources, grad, results, gl_o, gr_o, sem = refs[:5], refs[5], refs[6:11], *refs[11:]
    copies = [
        pltpu.make_async_copy(a, b, sem.at[n]) for n, (a, b) in enumerate(zip(sources, results))]
    for cp in copies:
        cp.start()
    for h in range(grad.shape[0] // HD):
        for n in range(grad.shape[1] // CB):
            block = grad[h * HD:(h + 1) * HD, n * CB:(n + 1) * CB]
            trace = jnp.sum(jnp.sum(block * block, axis=0, keepdims=True), axis=1, keepdims=True)
            inverse = 1.0 / (trace + epsilon)
            small = block.astype(BF16)
            gl_o[h, n] = dot_nt(small, small) * (inverse * HD)
            gr_o[h, n] = dot(block.T.astype(BF16), small) * (inverse * CB)
    for cp in copies:
        cp.wait()


def local(query_states, key_states, value_states, out_weight, upstream, tile_mask):
    nf = lax.axis_size("frame")
    nh = lax.axis_size("head")
    tok, hw = query_states.shape
    heads = hw // HD
    width = out_weight.shape[1]
    cols = width // nh
    cb = width // nf
    chips = nf // 2
    win = tile_mask.shape[1]
    reach = (win - 1) // 2
    halo = reach * TILE
    ext = tok + 2 * halo
    w_in = out_weight
    if cols % 128:
        w_in = out_weight.reshape(hw, nh, cols).transpose(1, 0, 2)
    up_in = upstream
    if cb % 128:
        up_in = upstream.reshape(tok, nf, cb).transpose(1, 0, 2)
    anywhere = pl.BlockSpec(memory_space=pl.ANY)
    vmem = pl.BlockSpec(memory_space=pltpu.VMEM)
    dma = pltpu.SemaphoreType.DMA
    *plain, grad = pl.pallas_call(
        functools.partial(kernel, nf, nh, tile_mask.shape[0]),
        out_shape=(
            jax.ShapeDtypeStruct((tok, hw), BF16),
            jax.ShapeDtypeStruct((tok, cols), BF16),
            jax.ShapeDtypeStruct((tok, hw), BF16),
            jax.ShapeDtypeStruct((tok, hw), BF16),
            jax.ShapeDtypeStruct((tok, hw), BF16),
            jax.ShapeDtypeStruct((hw, cb), F32),
        ),
        in_specs=[anywhere] * 6 + [pl.BlockSpec(memory_space=pltpu.SMEM)],
        out_specs=(anywhere,) * 6,
        scratch_shapes=[
            pltpu.VMEM((tok, hw), BF16),
            pltpu.VMEM((ext, hw), BF16),
            pltpu.VMEM((ext, hw), BF16),
            pltpu.VMEM((hw, width), BF16),
            pltpu.VMEM((nf, tok, cb), BF16),
            pltpu.VMEM((nh, hw, cols), BF16),
            pltpu.VMEM((nh, tok, hw), BF16),
            pltpu.VMEM((heads * (tok // TILE), win * TILE, TILE), BF16),
            pltpu.VMEM((hw, tok), BF16),
            pltpu.VMEM((tok, hw), BF16),
            pltpu.VMEM((hw, tok), BF16),
            pltpu.VMEM((hw, ext), BF16),
            pltpu.VMEM((hw, ext), BF16),
            pltpu.VMEM((ext, hw), F32),
            pltpu.VMEM((ext, hw), F32),
            pltpu.VMEM((2, 2, halo, hw), BF16),
            pltpu.VMEM((2, 2, halo, hw), BF16),
            pltpu.VMEM((3, tok, hw), BF16),
            pltpu.VMEM((tok, cols), BF16),
            pltpu.VMEM((chips, hw, cb), BF16),
            pltpu.VMEM((chips, hw, cb), BF16),
            pltpu.VMEM((hw, cb), F32),
            pltpu.VMEM((chips, hw, cb), BF16),
            pltpu.VMEM((chips, hw, cb), BF16),
            dma((5,)),
            dma((nf,)),
            dma((2, 2)), dma((2, 2)),
            dma((nh,)), dma((nh,)),
            dma((nh,)), dma((nh,)),
            dma((nh,)), dma((nh,)),
            dma((nh,)), dma((nh,)),
            dma((chips,)), dma((chips,)),
            dma((chips,)), dma((chips,)),
            dma((2,)), dma((2,)),
            dma((6,)),
        ],
        compiler_params=pltpu.CompilerParams(
            collective_id=0, has_side_effects=True, vmem_limit_bytes=56 * 1024 * 1024),
    )(query_states, key_states, value_states, out_weight, w_in, up_in, tile_mask.T)
    return pl.pallas_call(
        finish,
        out_shape=(
            *(jax.ShapeDtypeStruct(x.shape, x.dtype) for x in plain),
            jax.ShapeDtypeStruct((heads, cb // CB, HD, HD), F32),
            jax.ShapeDtypeStruct((heads, cb // CB, CB, CB), F32),
        ),
        in_specs=[anywhere] * 5 + [vmem],
        out_specs=(anywhere,) * 5 + (vmem, vmem),
        scratch_shapes=[dma((5,))],
        compiler_params=pltpu.CompilerParams(vmem_limit_bytes=60 * 1024 * 1024),
    )(*plain, grad)


def solution(mesh):
    return jax.shard_map(
        local,
        mesh=mesh,
        in_specs=(
            P("frame", "head"),
            P("frame", "head"),
            P("frame", "head"),
            P("head", None),
            P("frame", None),
            P(),
        ),
        out_specs=(
            P("frame", "head"),
            P("frame", "head"),
            P("frame", "head"),
            P("frame", "head"),
            P("frame", "head"),
            P("head", "frame", None, None),
            P("head", "frame", None, None),
        ),
        check_vma=False,
    )
```

```python
import functools
import math

import jax
import jax.numpy as jnp
from jax import lax
from jax.experimental import pallas as pl
from jax.experimental.pallas import tpu as pltpu
from jax.sharding import PartitionSpec as P

HD = 128
TILE = 256
CB = 320

epsilon = 1e-06
F32 = jnp.float32
BF16 = jnp.bfloat16
MESH = pl.DeviceIdType.MESH
NT = (((1,), (1,)), ((), ()))


def dot(a, b):
    return jnp.dot(a, b, preferred_element_type=F32)


def dot_nt(a, b):
    return lax.dot_general(a, b, NT, preferred_element_type=F32)


def kernel(
    nf, nh, tiles_all,
    q_hbm, k_hbm, v_hbm, w_hbm, wc_hbm, up_hbm, tm_ref,
    att_o, proj_o, dq_o, dk_o, dv_o, grad_o,
    qv, kext, vext, wv, upb, wcols, attall, wts, attT, ga, gaT,
    kT, vT, dkacc, dvacc, ghs, ghr, outs, projv, pa, sa, pb, sb, rb,
    load_sem, up_sem, halo_s, halo_r, w_s, w_r, tw_s, tw_r, fw_s, fw_r, at_s, at_r,
    sa_s, sa_r, rb_s, rb_r, gh_s, gh_r, out_sem,
):
    f = lax.axis_index("frame")
    hd = lax.axis_index("head")
    core = lax.rem(f, 2)
    chip = lax.div(f, 2)
    chips = nf // 2
    sib = f + 1 - 2 * core
    tok, hw = qv.shape
    heads = hw // HD
    qt = tok // TILE
    win = tm_ref.shape[0]
    reach = (win - 1) // 2
    halo = reach * TILE
    span = win * TILE
    half = hw // 2
    cols = wcols.shape[2]
    cb = upb.shape[2]
    scale = 1.0 / math.sqrt(HD)

    barrier = pltpu.get_barrier_semaphore()
    for d in range(1, nf):
        pl.semaphore_signal(barrier, inc=1, device_id=(lax.rem(f + d, nf), hd), device_id_type=MESH)
    for d in range(1, nh):
        pl.semaphore_signal(barrier, inc=1, device_id=(f, lax.rem(hd + d, nh)), device_id_type=MESH)

    def w_block(j, rows):
        if cols % 128 == 0:
            return w_hbm.at[rows, pl.ds(pl.multiple_of(j * cols, 128), cols)]
        return wc_hbm.at[j, rows]

    def up_block(j):
        if cb % 128 == 0:
            return up_hbm.at[:, pl.ds(j * cb, cb)]
        return up_hbm.at[j]

    center = pl.ds(halo, tok)
    loads = [
        pltpu.make_async_copy(w_hbm, wv, load_sem.at[0]),
        pltpu.make_async_copy(k_hbm, kext.at[center], load_sem.at[1]),
        pltpu.make_async_copy(v_hbm, vext.at[center], load_sem.at[2]),
        pltpu.make_async_copy(q_hbm, qv, load_sem.at[3]),
        pltpu.make_async_copy(w_block(hd, pl.ds(0, hw)), wcols.at[hd], load_sem.at[4]),
    ]
    ups = [pltpu.make_async_copy(up_block(j), upb.at[j], up_sem.at[j]) for j in range(nf)]
    loads[0].start()
    for cp in ups:
        cp.start()
    for cp in loads[1:]:
        cp.start()

    pl.semaphore_wait(barrier, nf + nh - 2)

    def halo_copy(side, which):
        src = (k_hbm, v_hbm)[which]
        dst = (kext, vext)[which]
        rows = pl.ds(0, halo) if side == 0 else pl.ds(halo + tok, halo)
        part = pl.ds(tok - halo, halo) if side == 0 else pl.ds(0, halo)
        to = f + 1 if side == 0 else f - 1
        return pltpu.make_async_remote_copy(
            src_ref=src.at[part], dst_ref=dst.at[rows],
            send_sem=halo_s.at[side, which], recv_sem=halo_r.at[side, which],
            device_id=(to, hd), device_id_type=MESH)

    has_next = f < nf - 1
    has_prev = f > 0

    for which in range(2):
        @pl.when(has_next)
        def _():
            halo_copy(0, which).start()

        @pl.when(has_prev)
        def _():
            halo_copy(1, which).start()

    my_rows = pl.ds(pl.multiple_of(core * half, half), half)
    quarter = half // 2
    upper_half = lax.div(f, nf // 2)
    other = lax.rem(f + nf // 2, nf)
    my_part = pl.ds(pl.multiple_of(core * half + upper_half * quarter, quarter), quarter)
    w_copies = []
    for d in range(1, nh):
        j = lax.rem(hd + d, nh)
        cp = pltpu.make_async_remote_copy(
            src_ref=w_block(j, my_part), dst_ref=wcols.at[hd, my_part],
            send_sem=w_s.at[d], recv_sem=w_r.at[d],
            device_id=(f, j), device_id_type=MESH)
        cp.start()
        w_copies.append(cp)

    @pl.when(jnp.logical_not(has_prev))
    def _():
        kext[pl.ds(0, halo)] = jnp.zeros((halo, hw), BF16)
        vext[pl.ds(0, halo)] = jnp.zeros((halo, hw), BF16)

    @pl.when(jnp.logical_not(has_next))
    def _():
        kext[pl.ds(halo + tok, halo)] = jnp.zeros((halo, hw), BF16)
        vext[pl.ds(halo + tok, halo)] = jnp.zeros((halo, hw), BF16)

    loads[0].wait()
    acc = None
    for j in range(nf):
        ups[j].wait()
        part = dot_nt(wv[:, j * cb:(j + 1) * cb], upb[j])
        acc = part if acc is None else acc + part
    gaT[...] = acc.astype(BF16)
    ga[...] = acc.T.astype(BF16)
    for cp in loads[1:]:
        cp.wait()

    def halo_arrived(which):
        @pl.when(has_prev)
        def _():
            halo_copy(0, which).wait_recv()

        @pl.when(has_next)
        def _():
            halo_copy(1, which).wait_recv()

    halo_arrived(0)

    def hcols(h):
        return pl.ds(h * HD, HD)

    for h in range(heads):
        for i in range(qt):
            rows = pl.ds(i * TILE, TILE)
            keys = pl.ds(i * TILE, span)
            s = dot_nt(kext[keys, hcols(h)], qv[rows, hcols(h)])
            parts = []
            tile = f * qt + i
            for o in range(win):
                b = tile + o - reach
                inside = jnp.where(jnp.logical_and(b >= 0, b < tiles_all), 1.0, 0.0)
                m = tm_ref[o, tile].astype(F32) * inside
                parts.append(s[o * TILE:(o + 1) * TILE] * (m * scale) + (m * 1e30 - 1e30))
            s = jnp.concatenate(parts, axis=0)
            p = jnp.exp(s - jnp.max(s, axis=0, keepdims=True))
            total = jnp.sum(p, axis=0, keepdims=True)
            wt = (p * (1.0 / total)).astype(BF16)
            wts[h * qt + i] = wt
    kT[...] = kext[...].T
    halo_arrived(1)
    vT[...] = vext[...].T
    for h in range(heads):
        for i in range(qt):
            rows = pl.ds(i * TILE, TILE)
            keys = pl.ds(i * TILE, span)
            attT[hcols(h), rows] = dot(vT[hcols(h), keys], wts[h * qt + i]).astype(BF16)
    attall[hd] = attT[...].T

    att_out = pltpu.make_async_copy(attall.at[hd], att_o, out_sem.at[0])
    att_out.start()
    at_copies = []
    for d in range(1, nh):
        cp = pltpu.make_async_remote_copy(
            src_ref=attall.at[hd], dst_ref=attall.at[hd],
            send_sem=at_s.at[d], recv_sem=at_r.at[d],
            device_id=(f, lax.rem(hd + d, nh)), device_id_type=MESH)
        cp.start()
        at_copies.append(cp)

    tw_copies = []
    for d in range(1, nh):
        w_copies[d - 1].wait_recv()
        s = lax.rem(hd + nh - d, nh)
        cp = pltpu.make_async_remote_copy(
            src_ref=wcols.at[s, my_part], dst_ref=wcols.at[s, my_part],
            send_sem=tw_s.at[d], recv_sem=tw_r.at[d],
            device_id=(other, hd), device_id_type=MESH)
        cp.start()
        tw_copies.append(cp)

    order = [*range(1, chips), 0]
    sa_copies = {}
    for d in order:
        q = lax.rem(chip + d, chips)
        pa[d] = dot(attT[...], upb[2 * q + 1 - core]).astype(BF16)
        cp = pltpu.make_async_remote_copy(
            src_ref=pa.at[d], dst_ref=sa.at[d], send_sem=sa_s.at[d], recv_sem=sa_r.at[d],
            device_id=(sib, hd), device_id_type=MESH)
        cp.start()
        sa_copies[d] = cp
    rb_copies = {}
    for d in order:
        q = lax.rem(chip + d, chips)
        part = dot(attT[...], upb[2 * q + core])
        sa_copies[d].wait_recv()
        part = part + sa[d].astype(F32)
        if d == 0:
            pb[...] = part
        else:
            sb[d] = part.astype(BF16)
            cp = pltpu.make_async_remote_copy(
                src_ref=sb.at[d], dst_ref=rb.at[d], send_sem=rb_s.at[d], recv_sem=rb_r.at[d],
                device_id=(2 * q + core, hd), device_id_type=MESH)
            cp.start()
            rb_copies[d] = cp

    dkacc[...] = jnp.zeros_like(dkacc)
    dvacc[...] = jnp.zeros_like(dvacc)
    for h in range(heads):
        for i in range(qt):
            rows = pl.ds(i * TILE, TILE)
            keys = pl.ds(i * TILE, span)
            wt = wts[h * qt + i]
            g = dot_nt(vext[keys, hcols(h)], ga[rows, hcols(h)])
            delta = jnp.sum(
                gaT[hcols(h), rows].astype(F32) * attT[hcols(h), rows].astype(F32),
                axis=0, keepdims=True)
            ds = (wt.astype(F32) * (g - delta)).astype(BF16)
            dqT = dot(kT[hcols(h), keys], ds) * scale
            outs[0, rows, hcols(h)] = dqT.T.astype(BF16)
            dkacc[keys, hcols(h)] += dot(ds, qv[rows, hcols(h)])
            dvacc[keys, hcols(h)] += dot(wt, ga[rows, hcols(h)])

    dq_out = pltpu.make_async_copy(outs.at[0], dq_o, out_sem.at[1])
    dq_out.start()

    def gh_copy(side):
        to = f + 1 if side == 0 else f - 1
        return pltpu.make_async_remote_copy(
            src_ref=ghs.at[side], dst_ref=ghr.at[side],
            send_sem=gh_s.at[side], recv_sem=gh_r.at[side],
            device_id=(to, hd), device_id_type=MESH)

    upper = pl.ds(halo + tok, halo)
    lower = pl.ds(0, halo)
    ghs[0, 0] = (dkacc[upper] * scale).astype(BF16)
    ghs[0, 1] = dvacc[upper].astype(BF16)
    ghs[1, 0] = (dkacc[lower] * scale).astype(BF16)
    ghs[1, 1] = dvacc[lower].astype(BF16)

    @pl.when(has_next)
    def _():
        gh_copy(0).start()

    @pl.when(has_prev)
    def _():
        gh_copy(1).start()

    @pl.when(jnp.logical_not(has_prev))
    def _():
        ghr[0] = jnp.zeros(ghr.shape[1:], BF16)

    @pl.when(jnp.logical_not(has_next))
    def _():
        ghr[1] = jnp.zeros(ghr.shape[1:], BF16)

    fw_copies = []
    for d in range(1, nh):
        tw_copies[d - 1].wait_recv()
        s = lax.rem(hd + nh - d, nh)
        cp = pltpu.make_async_remote_copy(
            src_ref=wcols.at[s, my_rows], dst_ref=wcols.at[s, my_rows],
            send_sem=fw_s.at[d], recv_sem=fw_r.at[d],
            device_id=(sib, hd), device_id_type=MESH)
        cp.start()
        fw_copies.append(cp)

    grad = pb[...]
    for d in range(1, chips):
        rb_copies[d].wait_recv()
        grad = grad + rb[d].astype(F32)
    pb[...] = grad
    grad_out = pltpu.make_async_copy(pb, grad_o, out_sem.at[5])
    grad_out.start()

    at_copies_all = at_copies
    acc = dot(attall[hd], wcols[hd])
    for d in range(1, nh):
        s = lax.rem(hd + nh - d, nh)
        at_copies_all[d - 1].wait_recv()
        fw_copies[d - 1].wait_recv()
        acc = acc + dot(attall[s], wcols[s])
    projv[...] = acc.astype(BF16)
    proj_out = pltpu.make_async_copy(projv, proj_o, out_sem.at[4])
    proj_out.start()

    @pl.when(has_prev)
    def _():
        gh_copy(0).wait_recv()

    @pl.when(has_next)
    def _():
        gh_copy(1).wait_recv()

    first, last = slice(0, halo), slice(tok - halo, tok)
    for which, (full, factor) in enumerate(((dkacc, scale), (dvacc, 1.0))):
        full[pl.ds(halo, halo)] += ghr[0, which].astype(F32) * (1.0 / factor)
        full[pl.ds(tok, halo)] += ghr[1, which].astype(F32) * (1.0 / factor)
        outs[1 + which] = (full[center] * factor).astype(BF16)
    dk_out = pltpu.make_async_copy(outs.at[1], dk_o, out_sem.at[2])
    dv_out = pltpu.make_async_copy(outs.at[2], dv_o, out_sem.at[3])
    dk_out.start()
    dv_out.start()

    for cp in (*w_copies, *tw_copies, *fw_copies, *at_copies, *sa_copies.values(), *rb_copies.values()):
        cp.wait_send()

    @pl.when(has_next)
    def _():
        for which in range(2):
            halo_copy(0, which).wait_send()
        gh_copy(0).wait_send()

    @pl.when(has_prev)
    def _():
        for which in range(2):
            halo_copy(1, which).wait_send()
        gh_copy(1).wait_send()

    for cp in (att_out, dq_out, dk_out, dv_out, proj_out, grad_out):
        cp.wait()


def finish(*refs):
    sources, grad_hbm, results, gl_o, gr_o = refs[:5], refs[5], refs[6:11], refs[11], refs[12]
    held, grad, in_sem, sem = refs[13:18], refs[18], refs[19], refs[20]
    grad_in = pltpu.make_async_copy(grad_hbm, grad, in_sem.at[5])
    grad_in.start()
    ins = [
        pltpu.make_async_copy(a, b, in_sem.at[n]) for n, (a, b) in enumerate(zip(sources, held))]
    copies = [
        pltpu.make_async_copy(a, b, sem.at[n]) for n, (a, b) in enumerate(zip(held, results))]
    for cp in ins:
        cp.start()
    for before, after in zip(ins, copies):
        before.wait()
        after.start()
    grad_in.wait()
    for h in range(grad.shape[0] // HD):
        for n in range(grad.shape[1] // CB):
            block = grad[h * HD:(h + 1) * HD, n * CB:(n + 1) * CB]
            trace = jnp.sum(jnp.sum(block * block, axis=0, keepdims=True), axis=1, keepdims=True)
            inverse = 1.0 / (trace + epsilon)
            small = block.astype(BF16)
            gl_o[h, n] = dot_nt(small, small) * (inverse * HD)
            gr_o[h, n] = dot(block.T.astype(BF16), small) * (inverse * CB)
    for cp in copies:
        cp.wait()


def local(query_states, key_states, value_states, out_weight, upstream, tile_mask):
    nf = lax.axis_size("frame")
    nh = lax.axis_size("head")
    tok, hw = query_states.shape
    heads = hw // HD
    width = out_weight.shape[1]
    cols = width // nh
    cb = width // nf
    chips = nf // 2
    win = tile_mask.shape[1]
    reach = (win - 1) // 2
    halo = reach * TILE
    ext = tok + 2 * halo
    w_in = out_weight
    if cols % 128:
        w_in = out_weight.reshape(hw, nh, cols).transpose(1, 0, 2)
    up_in = upstream
    if cb % 128:
        up_in = upstream.reshape(tok, nf, cb).transpose(1, 0, 2)
    anywhere = pl.BlockSpec(memory_space=pl.ANY)
    vmem = pl.BlockSpec(memory_space=pltpu.VMEM)
    dma = pltpu.SemaphoreType.DMA
    *plain, grad = pl.pallas_call(
        functools.partial(kernel, nf, nh, tile_mask.shape[0]),
        out_shape=(
            jax.ShapeDtypeStruct((tok, hw), BF16),
            jax.ShapeDtypeStruct((tok, cols), BF16),
            jax.ShapeDtypeStruct((tok, hw), BF16),
            jax.ShapeDtypeStruct((tok, hw), BF16),
            jax.ShapeDtypeStruct((tok, hw), BF16),
            jax.ShapeDtypeStruct((hw, cb), F32),
        ),
        in_specs=[anywhere] * 6 + [pl.BlockSpec(memory_space=pltpu.SMEM)],
        out_specs=(anywhere,) * 6,
        scratch_shapes=[
            pltpu.VMEM((tok, hw), BF16),
            pltpu.VMEM((ext, hw), BF16),
            pltpu.VMEM((ext, hw), BF16),
            pltpu.VMEM((hw, width), BF16),
            pltpu.VMEM((nf, tok, cb), BF16),
            pltpu.VMEM((nh, hw, cols), BF16),
            pltpu.VMEM((nh, tok, hw), BF16),
            pltpu.VMEM((heads * (tok // TILE), win * TILE, TILE), BF16),
            pltpu.VMEM((hw, tok), BF16),
            pltpu.VMEM((tok, hw), BF16),
            pltpu.VMEM((hw, tok), BF16),
            pltpu.VMEM((hw, ext), BF16),
            pltpu.VMEM((hw, ext), BF16),
            pltpu.VMEM((ext, hw), F32),
            pltpu.VMEM((ext, hw), F32),
            pltpu.VMEM((2, 2, halo, hw), BF16),
            pltpu.VMEM((2, 2, halo, hw), BF16),
            pltpu.VMEM((3, tok, hw), BF16),
            pltpu.VMEM((tok, cols), BF16),
            pltpu.VMEM((chips, hw, cb), BF16),
            pltpu.VMEM((chips, hw, cb), BF16),
            pltpu.VMEM((hw, cb), F32),
            pltpu.VMEM((chips, hw, cb), BF16),
            pltpu.VMEM((chips, hw, cb), BF16),
            dma((5,)),
            dma((nf,)),
            dma((2, 2)), dma((2, 2)),
            dma((nh,)), dma((nh,)),
            dma((nh,)), dma((nh,)),
            dma((nh,)), dma((nh,)),
            dma((nh,)), dma((nh,)),
            dma((chips,)), dma((chips,)),
            dma((chips,)), dma((chips,)),
            dma((2,)), dma((2,)),
            dma((6,)),
        ],
        compiler_params=pltpu.CompilerParams(
            collective_id=0, has_side_effects=True, vmem_limit_bytes=56 * 1024 * 1024),
    )(query_states, key_states, value_states, out_weight, w_in, up_in, tile_mask.T)
    return pl.pallas_call(
        finish,
        out_shape=(
            *(jax.ShapeDtypeStruct(x.shape, x.dtype) for x in plain),
            jax.ShapeDtypeStruct((heads, cb // CB, HD, HD), F32),
            jax.ShapeDtypeStruct((heads, cb // CB, CB, CB), F32),
        ),
        in_specs=[anywhere] * 6,
        out_specs=(anywhere,) * 5 + (vmem, vmem),
        scratch_shapes=[
            *(pltpu.VMEM(x.shape, x.dtype) for x in plain),
            pltpu.VMEM(grad.shape, F32),
            dma((6,)),
            dma((5,)),
        ],
        compiler_params=pltpu.CompilerParams(vmem_limit_bytes=60 * 1024 * 1024),
    )(*plain, grad)


def solution(mesh):
    return jax.shard_map(
        local,
        mesh=mesh,
        in_specs=(
            P("frame", "head"),
            P("frame", "head"),
            P("frame", "head"),
            P("head", None),
            P("frame", None),
            P(),
        ),
        out_specs=(
            P("frame", "head"),
            P("frame", "head"),
            P("frame", "head"),
            P("frame", "head"),
            P("frame", "head"),
            P("head", "frame", None, None),
            P("head", "frame", None, None),
        ),
        check_vma=False,
    )
```
